128 devices in a mesh: freq: 8 (over y, x_lo), row: 4 (over z), col: 4 (over x_hi, core).
Axes of the slice: x: 4 (x_hi: 2, x_lo: 2; x = x_hi * 2 + x_lo), y: 4, z: 4, core: 2. Of those that a mesh axis runs over, the one named last changes fastest.
Arguments:
- traces: float32 [512, 1024, 1024], P(('freq', 'row'), None, 'col'), may hold values from -6 to 6
Outputs:
- multiples: float32 [2, 32, 1024, 1024], P(None, 'freq', 'row', 'col')
The draws below stay inside these ranges and needn't reach their ends.
All inputs are finite; a program needn't handle non-finite values.
Results may differ from the reference program's by a relative error of at most 0.000098.
Values sent between devices are 32-bit elements; how exact they have to be, the bound alone decides.
No kernel may reach another device: no remote copies, remote signals or barrier semaphores. Data moves between devices by JAX's collectives and lax.ppermute only.
A program may use at most 128 MiB of HBM per device.

```python
import jax
import jax.numpy as jnp
from jax import lax

S = 1024
R = 1024
NT = 512
NF = 32


def block_scale(own_key, extent, split, low, largest):
    level, own = 1.0, jax.random.fold_in(own_key, 6)
    for position, parts in split:
        steps = jnp.exp(jax.random.uniform(jax.random.fold_in(own, position), (parts,), jnp.float32, low / len(split), largest / len(split)))
        level = level * jnp.repeat(steps, extent[position] // parts).reshape([-1 if axis == position else 1 for axis in range(len(extent))])
    return level


def noise(rng, extent, deviation, reach, split=(), kind=jnp.bfloat16):
    result = jax.random.normal(rng, extent, jnp.float32) * deviation
    if len(split) > 0:
        result = block_scale(rng, extent, split, -0.22, 0.18) * result
    return jnp.clip(result, min=-reach, max=reach).astype(kind)


def setup_inputs(seed: int = 0) -> dict:
    key_list = jax.random.split(jax.random.key(seed), 2)
    traces = noise(key_list[0], (NT, S, R), 1.0, 6.0, ((0, 32), (2, 4)), jnp.float32)
    return {"traces": traces}


def reference(traces):
    width = 32
    count = S // width

    def one_block(index):
        piece = lax.dynamic_slice_in_dim(traces, index * width, width, 1)
        wavefield_spectrum = jnp.fft.rfft(piece, axis=0)[1:NF + 1]
        return (jnp.real(wavefield_spectrum), jnp.imag(wavefield_spectrum))
    real_blocks, imag_blocks = lax.map(one_block, jnp.arange(count, dtype=jnp.int32))
    scale = 1.0 / jnp.sqrt(jnp.float32(NT))
    real_part = (jnp.transpose(real_blocks, (1, 0, 2, 3)).reshape(NF, S, R) * scale).astype(jnp.float32)
    imag_part = (jnp.transpose(imag_blocks, (1, 0, 2, 3)).reshape(NF, S, R) * scale).astype(jnp.float32)
    highest_precision = lax.Precision.HIGHEST

    def one_frequency(pair):
        pr, pi = pair
        output_real = jnp.dot(pr, pr, precision=highest_precision, preferred_element_type=jnp.float32) - jnp.dot(pi, pi, precision=highest_precision, preferred_element_type=jnp.float32)
        out_im = jnp.dot(pr, pi, precision=highest_precision, preferred_element_type=jnp.float32) + jnp.dot(pi, pr, precision=highest_precision, preferred_element_type=jnp.float32)
        return (output_real, out_im)
    output_real, out_im = lax.map(one_frequency, (real_part, imag_part))
    factor = 1.0 / jnp.sqrt(jnp.float32(S))
    return jnp.stack([output_real, out_im]) * factor
```

```python
import functools
import math

import jax
import jax.numpy as jnp
import numpy as np
from jax import lax
from jax.experimental import pallas as pl
from jax.experimental.pallas import tpu as pltpu
from jax.sharding import PartitionSpec as P

S = 1024
NT = 512
NF = 32
C = 256
PARTS = (("z", 0, 128), ("y", 128, 128))


def shift(x, axis, by):
    if axis == "z":
        return lax.ppermute(x, "row", [(i, (i + by) % 4) for i in range(4)])
    if axis == "y":
        return lax.ppermute(x, "freq", [(i, (i + 2 * by) % 8) for i in range(8)])
    if axis == "x_lo":
        return lax.ppermute(x, "freq", [(i, i ^ 1) for i in range(8)])
    if axis == "x_hi":
        return lax.ppermute(x, "col", [(i, i ^ 2) for i in range(4)])
    return lax.ppermute(x, "col", [(i, i ^ 1) for i in range(4)])


def dft_table():
    k = np.arange(NF) + 1
    phase = np.outer(k, np.arange(NT)) % NT * (2.0 * math.pi / NT)
    scale = 1.0 / math.sqrt(NT * math.sqrt(S))
    parts = np.stack([np.cos(phase), -np.sin(phase)]) * scale
    parts = parts.reshape(2, 8, 4, NT).transpose(1, 0, 2, 3)
    return parts.reshape(8, 8, NT).astype(np.float32)


def dft_kernel(rows, by_row, w_ref, *refs):
    pieces, outs = refs[:4], refs[4:]
    w = w_ref[...]
    wh = w.astype(jnp.bfloat16)
    wl = (w - wh.astype(jnp.float32)).astype(jnp.bfloat16)
    wcat = jnp.concatenate([wh, wh, wl], axis=1)
    for s in range(rows):
        x = jnp.concatenate([p[:, s, :] for p in pieces], axis=0)
        xh = x.astype(jnp.bfloat16)
        xl = (x - xh.astype(jnp.float32)).astype(jnp.bfloat16)
        xcat = jnp.concatenate([xh, xl, xh], axis=0)
        res = jnp.dot(wcat, xcat, preferred_element_type=jnp.float32)
        if by_row:
            for q in range(2):
                outs[q][:, s, :] = res[32 * q : 32 * q + 32]
        else:
            for i in range(8):
                outs[i][:, s, :] = res[8 * i : 8 * i + 8]


def dft(kind, pieces, w):
    rows = pieces[0].shape[1]
    by_row = kind == "y"
    if by_row:
        quarter = rows // 4
        result = []
        for r in range(4):
            result.append(
                pl.pallas_call(
                    functools.partial(dft_kernel, quarter, True),
                    grid=(1,),
                    in_specs=[pl.BlockSpec((64, 64), lambda g: (0, 0))]
                    + [pl.BlockSpec((16, quarter, C), lambda g, r=r: (0, r, 0))] * 4,
                    out_specs=[pl.BlockSpec((32, quarter, C), lambda g: (0, 0, 0))] * 2,
                    out_shape=[jax.ShapeDtypeStruct((32, quarter, C), jnp.float32)] * 2,
                    compiler_params=pltpu.CompilerParams(vmem_limit_bytes=48 << 20),
                )(w, *pieces)
            )
        return result
    block = 16
    flat = pl.pallas_call(
        functools.partial(dft_kernel, block, False),
        grid=(rows // block,),
        in_specs=[pl.BlockSpec((64, 64), lambda g: (0, 0))]
        + [pl.BlockSpec((16, block, C), lambda g: (0, g, 0))] * 4,
        out_specs=[pl.BlockSpec((8, block, C), lambda g: (0, g, 0))] * 8,
        out_shape=[jax.ShapeDtypeStruct((8, rows, C), jnp.float32)] * 8,
        compiler_params=pltpu.CompilerParams(vmem_limit_bytes=48 << 20),
    )(w, *pieces)
    return [flat[2 * r : 2 * r + 2] for r in range(4)]


def reduce_ring(slots, axis):
    up0 = shift(slots[2][0], axis, 1)
    down1 = shift(slots[2][1], axis, -1)
    up1 = shift(slots[1][1], axis, 1)
    down0 = shift(slots[3][0], axis, -1)
    up0 = shift(slots[1][0] + up0, axis, 1)
    down1 = shift(slots[3][1] + down1, axis, -1)
    return [slots[0][0] + up0 + down0, slots[0][1] + up1 + down1]


def gather_ring(x, axis):
    below = shift(x, axis, 1)
    above = shift(x, axis, -1)
    first = shift(below[:4], axis, 1)
    second = shift(above[4:], axis, -1)
    return [[x], [above], [first, second], [below]]


def local(x):
    f = lax.axis_index("freq")
    y, x_lo = f // 2, f % 2
    z = lax.axis_index("row")
    col = lax.axis_index("col")

    table = jnp.asarray(dft_table())
    owners = [[2 * ((y + r) % 4) + (x_lo + q) % 2 for q in range(2)] for r in range(4)]
    rows_of = [[lax.dynamic_index_in_dim(table, o, 0, False) for o in pair] for pair in owners]
    for_z = jnp.concatenate([rows_of[r][q] for r in range(4) for q in range(2)])
    for_y = jnp.concatenate([rows_of[r][q] for q in range(2) for r in range(4)])

    def times(w, starts):
        return jnp.concatenate([lax.dynamic_slice_in_dim(w, t, 16, 1) for t in starts], axis=1)

    w_z = times(for_z, [64 * f + 16 * ((z + 4 - r) % 4) for r in range(4)])
    w_y = times(for_y, [128 * ((y + 4 - r) % 4) + 64 * x_lo + 16 * z for r in range(4)])

    def rows(start, size):
        return lax.dynamic_slice_in_dim(x, start, size, 1)

    pieces = []
    for kind, start, size in PARTS:
        got = []
        for r in range(4):
            if kind == "z":
                piece = rows(256 * ((z + r) % 4) + start, size)
            else:
                quarter = size // 4
                inner = start + quarter * ((y + r) % 4)
                piece = jnp.concatenate([rows(256 * ((z + s) % 4) + inner, quarter) for s in range(4)], axis=1)
            got.append(piece if r == 0 else shift(piece, kind, r))
        pieces.append(got)

    own = []
    for (kind, start, size), got in zip(PARTS, pieces):
        slots = dft(kind, got, w_z if kind == "z" else w_y)
        mine, other = reduce_ring(slots, "y" if kind == "z" else "z")
        total = mine + shift(other, "x_lo", 1)
        if kind == "y":
            quarter = size // 4
            total = total.reshape(4, 8, quarter, C)
            whole = jnp.zeros((8, size, C), jnp.float32)
            for r in range(4):
                piece = total[r] if r == 0 else shift(total[r], "y", r)
                at = quarter * ((y + 4 - r) % 4)
                whole = lax.dynamic_update_slice(whole, piece, (0, at, 0))
            total = whole
        own.append(total)

    right = jnp.zeros((8, S, C), jnp.float32)
    for (kind, start, size), block in zip(PARTS, own):
        for r, got in enumerate(gather_ring(block, "z")):
            at = 256 * ((z + r) % 4) + start
            for i, piece in enumerate(got):
                right = lax.dynamic_update_slice(right, piece, (4 * i, at, 0))

    block = jnp.concatenate(own, axis=1)
    far = shift(block, "x_hi", 1)
    near, near_far = shift(block, "core", 1), shift(far, "core", 1)
    left = jnp.zeros((8, 256, S), jnp.float32)
    for piece, c in ((block, col), (near, col ^ 1), (far, col ^ 2), (near_far, col ^ 3)):
        left = lax.dynamic_update_slice(left, piece, (0, 0, 256 * c))

    ar, ai, br, bi = left[:4], left[4:], right[:4], right[4:]
    dot = functools.partial(
        jnp.einsum, "gik,gkj->gij", precision=lax.Precision.HIGH, preferred_element_type=jnp.float32
    )
    return jnp.stack([dot(ar, br) - dot(ai, bi), dot(ar, bi) + dot(ai, br)])


def solution(mesh):
    in_specs = (P(("freq", "row"), None, "col"),)
    out_specs = P(None, "freq", "row", "col")
    return jax.shard_map(local, mesh=mesh, in_specs=in_specs, out_specs=out_specs, check_vma=False)
```

```python
import functools
import math

import jax
import jax.numpy as jnp
import numpy as np
from jax import lax
from jax.experimental import pallas as pl
from jax.experimental.pallas import tpu as pltpu
from jax.sharding import PartitionSpec as P

S = 1024
NT = 512
NF = 32
C = 256
R1, R2, R3 = 96, 64, 96
VMEM = 50 << 20


def shift(x, axis, by=1):
    if axis == "z":
        return lax.ppermute(x, "row", [(i, (i + by) % 4) for i in range(4)])
    if axis == "y":
        return lax.ppermute(x, "freq", [(i, (i + 2 * by) % 8) for i in range(8)])
    if axis == "x_lo":
        return lax.ppermute(x, "freq", [(i, i ^ 1) for i in range(8)])
    if axis == "x_hi":
        return lax.ppermute(x, "col", [(i, i ^ 2) for i in range(4)])
    return lax.ppermute(x, "col", [(i, i ^ 1) for i in range(4)])


def together(*values):
    return lax.optimization_barrier(values)


def tables():
    k = np.arange(NF) + 1
    phase = np.outer(k, np.arange(NT)) % NT * (2.0 * math.pi / NT)
    scale = 1.0 / math.sqrt(NT * math.sqrt(S))
    full = np.stack([np.cos(phase), -np.sin(phase)]) * scale
    full = full.reshape(2, 8, 4, NT).transpose(1, 0, 2, 3).reshape(8, 8, NT).astype(np.float32)
    one, two, three = [], [], []
    u = np.arange(16)
    for f in range(8):
        y, x_lo = f // 2, f % 2
        owner = np.array([[2 * ((y + ry) % 4) + (x_lo + q) % 2 for q in range(2)] for ry in range(4)])
        by_y = full[owner.reshape(-1)].reshape(64, NT)
        by_q = full[owner.T.reshape(-1)].reshape(64, NT)
        near, far = 64 * f + np.arange(64), 64 * (f ^ 1) + np.arange(64)
        one.append(by_y[:, near])
        three.append(by_y[:, np.stack([near.reshape(4, 16), far.reshape(4, 16)], axis=1).reshape(-1)])
        for z in range(4):
            t = [128 * ((y - r) % 4) + 64 * x_lo + 16 * z + u for r in range(4)]
            two.append(by_q[:, np.concatenate(t)])
    return np.stack(one), np.stack(two), np.stack(three)


def cost(us):
    return pl.CostEstimate(flops=0, bytes_accessed=int(us * 3.6e6), transcendentals=0)


def transform(w_ref, samples, store, rows):
    w = w_ref[0]
    wh = w.astype(jnp.bfloat16)
    wl = (w - wh.astype(jnp.float32)).astype(jnp.bfloat16)
    wcat = jnp.concatenate([wh, wh, wl], axis=1)
    for s in range(rows):
        x = samples(s)
        xh = x.astype(jnp.bfloat16)
        xl = (x - xh.astype(jnp.float32)).astype(jnp.bfloat16)
        xcat = jnp.concatenate([xh, xl, xh], axis=0)
        store(s, jnp.dot(wcat, xcat, preferred_element_type=jnp.float32))


def dft_owner_kernel(rows, _, w_ref, x_ref, *outs):
    def samples(s):
        return jnp.concatenate([x_ref[j, :, s, :] for j in range(x_ref.shape[0])], axis=0)

    def store(s, res):
        for i in range(8):
            outs[i][:, s, :] = res[8 * i : 8 * i + 8]

    transform(w_ref, samples, store, rows)


def dft_by_owner(index, w, x, block):
    n, _, rows, _ = x.shape
    k = w.shape[2]
    flat = pl.pallas_call(
        functools.partial(dft_owner_kernel, block),
        grid_spec=pltpu.PrefetchScalarGridSpec(
            num_scalar_prefetch=1,
            grid=(rows // block,),
            in_specs=[
                pl.BlockSpec((1, 64, k), lambda g, i: (i[0], 0, 0)),
                pl.BlockSpec((n, 16, block, C), lambda g, i: (0, 0, g, 0)),
            ],
            out_specs=[pl.BlockSpec((8, block, C), lambda g, i: (0, g, 0))] * 8,
        ),
        out_shape=[jax.ShapeDtypeStruct((8, rows, C), jnp.float32)] * 8,
        compiler_params=pltpu.CompilerParams(vmem_limit_bytes=VMEM),
        cost_estimate=cost(12),
    )(index, w, x)
    return [flat[2 * r : 2 * r + 2] for r in range(4)]


def dft_row_kernel(rows, _, w_ref, *refs):
    pieces, outs = refs[:4], refs[4:]

    def samples(s):
        return jnp.concatenate([p[:, 0, s, :] for p in pieces], axis=0)

    def store(s, res):
        for q in range(2):
            outs[q][0, :, s, :] = res[32 * q : 32 * q + 32]

    transform(w_ref, samples, store, rows)


def dft_by_row(index, w, pieces):
    rows = pieces[0].shape[2]
    return pl.pallas_call(
        functools.partial(dft_row_kernel, rows),
        grid_spec=pltpu.PrefetchScalarGridSpec(
            num_scalar_prefetch=1,
            grid=(4,),
            in_specs=[pl.BlockSpec((1, 64, 64), lambda g, i: (i[0], 0, 0))]
            + [pl.BlockSpec((16, 1, rows, C), lambda g, i: (0, g, 0, 0))] * 4,
            out_specs=[pl.BlockSpec((1, 32, rows, C), lambda g, i: (g, 0, 0, 0))] * 2,
        ),
        out_shape=[jax.ShapeDtypeStruct((4, 32, rows, C), jnp.float32)] * 2,
        compiler_params=pltpu.CompilerParams(vmem_limit_bytes=VMEM),
        cost_estimate=cost(7),
    )(index, w, *pieces)


def reduce_ring(slots, axis):
    up0 = shift(slots[2][0], axis, 1)
    down1 = shift(slots[2][1], axis, -1)
    up1 = shift(slots[1][1], axis, 1)
    down0 = shift(slots[3][0], axis, -1)
    up0 = shift(slots[1][0] + up0, axis, 1)
    down1 = shift(slots[3][1] + down1, axis, -1)
    return [slots[0][0] + up0 + down0, slots[0][1] + up1 + down1]


def product_kernel(starts, sizes, index, *refs):
    n = len(starts)
    left, right = refs[: 8 * n], refs[8 * n : 10 * n]
    out, a_ref, b_ref = refs[10 * n :]
    col = index[0]

    def split(x):
        hi = x.astype(jnp.bfloat16)
        return hi, (x - hi.astype(jnp.float32)).astype(jnp.bfloat16)

    for i in range(n):
        rows = slice(starts[i], starts[i] + sizes[i])
        for part in range(2):
            for e in range(4):
                hi, lo = split(left[8 * i + 2 * e + part][0])
                a_ref[col ^ e, 2 * part, rows] = hi
                a_ref[col ^ e, 2 * part + 1, rows] = lo
            for k in range(4):
                hi, lo = split(right[2 * i + part][k, 0])
                b_ref[k, 2 * part, rows] = hi
                b_ref[k, 2 * part + 1, rows] = lo

    def dot(x, y):
        return jnp.dot(x, y, preferred_element_type=jnp.float32)

    rr = jnp.zeros((256, C), jnp.float32)
    ii, ri, ir = rr, rr, rr
    for k in range(4):
        arh, arl, aih, ail = (a_ref[k, j] for j in range(4))
        brh, brl, bih, bil = (b_ref[k, j] for j in range(4))
        rr += dot(arh, brh) + dot(arh, brl) + dot(arl, brh)
        ii += dot(aih, bih) + dot(aih, bil) + dot(ail, bih)
        ri += dot(arh, bih) + dot(arh, bil) + dot(arl, bih)
        ir += dot(aih, brh) + dot(aih, brl) + dot(ail, brh)
    out[0, 0] = rr - ii
    out[1, 0] = ri + ir


def product(index, left, right, starts, sizes):
    operands, specs = [], []
    for i, part in enumerate(left):
        for block in part:
            operands += [block, block]
            specs += [pl.BlockSpec((1, sizes[i], C), lambda g, _, p=p: (p + g, 0, 0)) for p in (0, 4)]
    for i, part in enumerate(right):
        operands += [part, part]
        specs += [pl.BlockSpec((4, 1, sizes[i], C), lambda g, _, p=p: (0, p + g, 0, 0)) for p in (0, 4)]
    return pl.pallas_call(
        functools.partial(product_kernel, starts, sizes),
        grid_spec=pltpu.PrefetchScalarGridSpec(
            num_scalar_prefetch=1,
            grid=(4,),
            in_specs=specs,
            out_specs=pl.BlockSpec((2, 1, 256, C), lambda g, i: (0, g, 0, 0)),
            scratch_shapes=[
                pltpu.VMEM((4, 4, 256, C), jnp.bfloat16),
                pltpu.VMEM((4, 4, 256, C), jnp.bfloat16),
            ],
        ),
        out_shape=jax.ShapeDtypeStruct((2, 4, 256, C), jnp.float32),
        compiler_params=pltpu.CompilerParams(vmem_limit_bytes=VMEM),
        cost_estimate=cost(13),
    )(index, *operands)


def local(x):
    f = lax.axis_index("freq")
    y, x_lo = f // 2, f % 2
    z = lax.axis_index("row")
    col = lax.axis_index("col")
    one, two, three = tables()
    at_f = jnp.stack([f])
    blocks = x.reshape(16, 4, 256, C)

    def rows(start, size):
        return lax.dynamic_slice_in_dim(blocks, start, size, 2)

    quarter, half = R2 // 4, R3 // 2
    first = jnp.transpose(blocks[:, :, :R1], (1, 0, 2, 3))
    first = lax.all_to_all(first, "row", split_axis=0, concat_axis=0, tiled=True)
    third_own, third_far = rows(R1 + R2 + half * x_lo, half), rows(R1 + R2 + half * (1 - x_lo), half)
    third_far = shift(third_far, "x_lo")
    second = [rows(R1 + quarter * ((y + r) % 4), quarter) for r in range(4)]
    second = [second[0]] + [shift(second[r], "y", r) for r in (1, 2, 3)]
    first, third_own, third_far, second = together(first, third_own, third_far, second)

    third = jnp.transpose(jnp.stack([third_own, third_far]), (2, 0, 1, 3, 4))
    third = lax.all_to_all(third, "row", split_axis=0, concat_axis=0, tiled=True)
    slots = dft_by_owner(at_f, one, first, 16)
    mine2, other2 = dft_by_row(jnp.stack([4 * f + z]), two, second)
    slots, mine2, other2 = together(slots, mine2, other2)
    mine1, other1 = reduce_ring(slots, "y")
    own2 = mine2 + shift(other2, "x_lo")
    mine1, other1, own2, third = together(mine1, other1, own2, third)

    slots = dft_by_owner(at_f, three, third.reshape(8, 16, half, C), 16)
    own1 = mine1 + shift(other1, "x_lo")
    own2 = lax.psum_scatter(own2, "row", scatter_dimension=0, tiled=False)
    mine3, other3 = reduce_ring(slots, "y")
    own1, own2, mine3, other3 = together(own1, own2, mine3, other3)

    bins = [own2[8 * r : 8 * r + 8] for r in range(4)]
    own2 = jnp.zeros((8, R2, C), jnp.float32)
    for r in range(4):
        piece = bins[r] if r == 0 else shift(bins[r], "y", r)
        own2 = lax.dynamic_update_slice(own2, piece, (0, quarter * ((y + 4 - r) % 4), 0))
    other3 = shift(other3, "x_lo")
    own3 = jnp.where(x_lo == 0, jnp.concatenate([mine3, other3], axis=1), jnp.concatenate([other3, mine3], axis=1))
    rest = jnp.concatenate([own2, own3], axis=1)

    left, right = [], []
    for part in (own1, rest):
        far = shift(part, "x_hi")
        right.append(lax.all_gather(part, "row", axis=0, tiled=False))
        left.append((part, shift(part, "core"), far, shift(far, "core")))
    return product(jnp.stack([col]), left, right, (0, R1), (R1, R2 + R3))


def solution(mesh):
    in_specs = (P(("freq", "row"), None, "col"),)
    out_specs = P(None, "freq", "row", "col")
    return jax.shard_map(local, mesh=mesh, in_specs=in_specs, out_specs=out_specs, check_vma=False)
```

```python
import functools
import math

import jax
import jax.numpy as jnp
import numpy as np
from jax import lax
from jax.experimental import pallas as pl
from jax.experimental.pallas import tpu as pltpu
from jax.sharding import PartitionSpec as P

S = 1024
NT = 512
NF = 32
C = 256
R3, R2, R1 = 96, 64, 96
HALF, QUARTER = R3 // 2, R2 // 4
VMEM = 50 << 20


def shift(x, axis, by=1):
    if axis == "z":
        return lax.ppermute(x, "row", [(i, (i + by) % 4) for i in range(4)])
    if axis == "y":
        return lax.ppermute(x, "freq", [(i, (i + 2 * by) % 8) for i in range(8)])
    if axis == "x_lo":
        return lax.ppermute(x, "freq", [(i, i ^ 1) for i in range(8)])
    if axis == "x_hi":
        return lax.ppermute(x, "col", [(i, i ^ 2) for i in range(4)])
    return lax.ppermute(x, "col", [(i, i ^ 1) for i in range(4)])


def exchange(x, axis):
    if axis == "z":
        return lax.all_to_all(x, "row", split_axis=0, concat_axis=0, tiled=True)
    groups = [[2 * j + i for j in range(4)] for i in range(2)]
    return lax.all_to_all(x, "freq", split_axis=0, concat_axis=0, tiled=True, axis_index_groups=groups)


def together(*values):
    return lax.optimization_barrier(values)


def cost(us):
    return pl.CostEstimate(flops=0, bytes_accessed=int(us * 3.6e6), transcendentals=0)


def call(kernel, index, operands, grid, in_specs, out_specs, out_shape, us, scratch_shapes=()):
    return pl.pallas_call(
        kernel,
        grid_spec=pltpu.PrefetchScalarGridSpec(
            num_scalar_prefetch=1, grid=grid, in_specs=in_specs, out_specs=out_specs, scratch_shapes=scratch_shapes
        ),
        out_shape=out_shape,
        compiler_params=pltpu.CompilerParams(vmem_limit_bytes=VMEM),
        cost_estimate=cost(us),
    )(index, *operands)


def f32(*shape):
    return jax.ShapeDtypeStruct(shape, jnp.float32)


def tables():
    k = np.arange(NF) + 1
    phase = np.outer(k, np.arange(NT)) % NT * (2.0 * math.pi / NT)
    scale = 1.0 / math.sqrt(NT * math.sqrt(S))
    full = np.stack([np.cos(phase), -np.sin(phase)]) * scale
    full = full.reshape(2, 8, 4, NT).transpose(1, 0, 2, 3).reshape(8, 8, NT).astype(np.float32)
    one, two, three = [], [], []
    u = np.arange(16)
    for f in range(8):
        y, x_lo = f // 2, f % 2
        by_y = [2 * ((y + ry) % 4) + (x_lo + q) % 2 for ry in range(4) for q in range(2)]
        by_q = [2 * y_to + (x_lo + q) % 2 for q in range(2) for y_to in range(4)]
        by_y, by_q = full[by_y].reshape(64, NT), full[by_q].reshape(64, NT)
        near, far = 64 * f + np.arange(64), 64 * (f ^ 1) + np.arange(64)
        one.append(by_y[:, near])
        three.append(by_y[:, np.stack([near.reshape(4, 16), far.reshape(4, 16)], axis=1).reshape(-1)])
        for z in range(4):
            t = [128 * ((y - r) % 4) + 64 * x_lo + 16 * z + u for r in range(4)]
            two.append(by_q[:, np.concatenate(t)])
    return np.stack(one), np.stack(two), np.stack(three)


def staged(pairs, stage_ref, in_sem, out_sem):
    ins = [pltpu.make_async_copy(a, stage_ref.at[n], in_sem.at[n]) for n, (a, _) in enumerate(pairs)]
    outs = [pltpu.make_async_copy(stage_ref.at[n], b, out_sem.at[n]) for n, (_, b) in enumerate(pairs)]
    for copy in ins:
        copy.start()
    for copy_in, copy_out in zip(ins, outs):
        copy_in.wait()
        copy_out.start()
    for copy in outs:
        copy.wait()


def pack_kernel(index, x_ref, out_ref, *scratch, views):
    staged(views(index, x_ref, out_ref), *scratch)


def stage(n, shape):
    return [pltpu.VMEM((n, *shape), jnp.float32), pltpu.SemaphoreType.DMA((n,)), pltpu.SemaphoreType.DMA((n,))]


def pack(index, blocks, views, n, piece, shape, us):
    anywhere = pl.BlockSpec(memory_space=pl.ANY)
    return call(
        functools.partial(pack_kernel, views=views),
        index,
        (blocks,),
        (1,),
        [anywhere],
        anywhere,
        f32(*shape),
        us,
        stage(n, piece),
    )


def join_kernel(far_ref, joined_ref, out_ref, *scratch):
    del joined_ref
    staged([(far_ref.at[g], out_ref.at[g, 1]) for g in range(4)], *scratch)


def join(joined, far):
    anywhere = pl.BlockSpec(memory_space=pl.ANY)
    return pl.pallas_call(
        join_kernel,
        in_specs=[anywhere] * 2,
        out_specs=anywhere,
        out_shape=f32(*joined.shape),
        scratch_shapes=stage(4, far.shape[1:]),
        input_output_aliases={1: 0},
        compiler_params=pltpu.CompilerParams(vmem_limit_bytes=VMEM),
        cost_estimate=cost(3),
    )(far, joined)


def rows_at(start, size):
    return pl.ds(pl.multiple_of(start, 8), size)


def transform(w_ref, samples, store, rows):
    w = w_ref[0]
    wh = w.astype(jnp.bfloat16)
    wl = (w - wh.astype(jnp.float32)).astype(jnp.bfloat16)
    wcat = jnp.concatenate([wh, wh, wl], axis=1)
    for s in range(rows):
        x = samples(s)
        xh = x.astype(jnp.bfloat16)
        xl = (x - xh.astype(jnp.float32)).astype(jnp.bfloat16)
        xcat = jnp.concatenate([xh, xl, xh], axis=0)
        store(s, jnp.dot(wcat, xcat, preferred_element_type=jnp.float32))


def dft_owner_kernel(rows, _, w_ref, x_ref, *outs):
    def samples(s):
        return jnp.concatenate([x_ref[j, :, s, :] for j in range(x_ref.shape[0])], axis=0)

    def store(s, res):
        for i, out in enumerate(outs):
            out[:, s, :] = res[8 * i : 8 * i + 8]

    transform(w_ref, samples, store, rows)


def dft_by_owner(index, w, x, us):
    n, _, rows, _ = x.shape
    block = 16
    flat = call(
        functools.partial(dft_owner_kernel, block),
        index,
        (w, x),
        (rows // block,),
        [
            pl.BlockSpec((1, 64, w.shape[2]), lambda g, i: (i[0], 0, 0)),
            pl.BlockSpec((n, 16, block, C), lambda g, i: (0, 0, g, 0)),
        ],
        [pl.BlockSpec((8, block, C), lambda g, i: (0, g, 0))] * 8,
        [f32(8, rows, C)] * 8,
        us,
    )
    return [flat[2 * r : 2 * r + 2] for r in range(4)]


def dft_row_kernel(rows, _, w_ref, *refs):
    pieces, outs = refs[:4], refs[4:]

    def samples(s):
        return jnp.concatenate([p[:, 0, s, :] for p in pieces], axis=0)

    def store(s, res):
        for q in range(2):
            outs[q][0, :, s, :] = res[32 * q : 32 * q + 32]

    transform(w_ref, samples, store, rows)


def dft_by_row(index, w, blocks, pieces):
    at = R3 // QUARTER
    return call(
        functools.partial(dft_row_kernel, QUARTER),
        index,
        (w, blocks, *pieces),
        (4,),
        [
            pl.BlockSpec((1, 64, 64), lambda g, i: (i[0], 0, 0)),
            pl.BlockSpec((16, 1, QUARTER, C), lambda g, i: (0, g, at + i[1], 0)),
        ]
        + [pl.BlockSpec((16, 1, QUARTER, C), lambda g, i: (0, g, 0, 0))] * 3,
        [pl.BlockSpec((1, 32, QUARTER, C), lambda g, i: (g, 0, 0, 0))] * 2,
        [f32(4, 32, QUARTER, C)] * 2,
        7,
    )


def reduce_ring(slots, axis):
    up0 = shift(slots[2][0], axis, 1)
    down1 = shift(slots[2][1], axis, -1)
    up1 = shift(slots[1][1], axis, 1)
    down0 = shift(slots[3][0], axis, -1)
    up0 = shift(slots[1][0] + up0, axis, 1)
    down1 = shift(slots[3][1] + down1, axis, -1)
    return [slots[0][0] + up0 + down0, slots[0][1] + up1 + down1]


def near_z(x):
    return shift(x, "z", 1), shift(x, "z", -1)


def across_z(below, above):
    return shift(below[:4], "z", 1), shift(above[4:], "z", -1)


def split(x):
    hi = x.astype(jnp.bfloat16)
    return hi, (x - hi.astype(jnp.float32)).astype(jnp.bfloat16)


def dots(a, b, out, total):
    def dot(x, y):
        return jnp.dot(x, y, preferred_element_type=jnp.float32)

    rr, ri = total
    ii, ir = jnp.zeros((256, C), jnp.float32), jnp.zeros((256, C), jnp.float32)
    for (arh, arl, aih, ail), (brh, brl, bih, bil) in zip(a, b):
        rr += dot(arh, brh) + dot(arh, brl) + dot(arl, brh)
        ii += dot(aih, bih) + dot(aih, bil) + dot(ail, bih)
        ri += dot(arh, bih) + dot(arh, bil) + dot(arl, bih)
        ir += dot(aih, brh) + dot(aih, brl) + dot(ail, brh)
    out[0, 0] = rr - ii
    out[1, 0] = ri + ir


def near_kernel(segments, index, *refs):
    n = len(segments)
    left, right = refs[: 8 * n], refs[8 * n : 14 * n]
    out, kept, a_ref, b_ref = refs[14 * n :]
    col, z = index[0], index[1]
    for i, rows in enumerate(segments):
        for part in range(2):
            for e in range(4):
                hi, lo = split(left[8 * i + 2 * e + part][0])
                a_ref[col ^ e, 2 * part, rows] = hi
                a_ref[col ^ e, 2 * part + 1, rows] = lo
            for t in range(3):
                hi, lo = split(right[6 * i + 2 * t + part][0])
                b_ref[t, 2 * part, rows] = hi
                b_ref[t, 2 * part + 1, rows] = lo
    zero = jnp.zeros((256, C), jnp.float32)
    a = [[a_ref[(z + r) % 4, j] for j in range(4)] for r in (0, 1, 3)]
    dots(a, [[b_ref[t, j] for j in range(4)] for t in range(3)], out, (zero, zero))
    kept[0] = a_ref[(z + 2) % 4]


def far_kernel(segments, _, total, kept, *refs):
    out, b_ref = refs[-2:]
    for i, rows in enumerate(segments):
        for part in range(2):
            hi, lo = split(refs[2 * i + part][0])
            b_ref[2 * part, rows] = hi
            b_ref[2 * part + 1, rows] = lo
    a, b = [kept[0, j] for j in range(4)], [b_ref[j] for j in range(4)]
    dots([a], [b], out, (total[0, 0], total[1, 0]))


def product(index, left, right, across, starts):
    sizes = [part[0].shape[1] for part in left]
    segments = [slice(a, a + b) for a, b in zip(starts, sizes)]

    def spec(rows, first):
        return pl.BlockSpec((1, rows, C), lambda g, _: (first + g, 0, 0))

    def both(groups):
        operands, specs = [], []
        for arrays, rows in zip(groups, sizes):
            for array in arrays:
                operands += [array, array]
                specs += [spec(rows, 0), spec(rows, 4)]
        return operands, specs

    left, left_specs = both(left)
    right, right_specs = both(right)
    out_spec = pl.BlockSpec((2, 1, 256, C), lambda g, _: (0, g, 0, 0))
    kept_spec = pl.BlockSpec((1, 4, 256, C), lambda g, _: (g, 0, 0, 0))
    total, kept = call(
        functools.partial(near_kernel, segments),
        index,
        left + right,
        (4,),
        left_specs + right_specs,
        [out_spec, kept_spec],
        [f32(2, 4, 256, C), jax.ShapeDtypeStruct((4, 4, 256, C), jnp.bfloat16)],
        11,
        [pltpu.VMEM((4, 4, 256, C), jnp.bfloat16), pltpu.VMEM((3, 4, 256, C), jnp.bfloat16)],
    )
    return call(
        functools.partial(far_kernel, segments),
        index,
        [total, kept] + [array for pair in across for array in pair],
        (4,),
        [out_spec, kept_spec] + [spec(rows, 0) for rows in sizes for _ in range(2)],
        out_spec,
        f32(2, 4, 256, C),
        4,
        [pltpu.VMEM((4, 256, C), jnp.bfloat16)],
    )


def local(x):
    f = lax.axis_index("freq")
    y, x_lo = f // 2, f % 2
    z = lax.axis_index("row")
    col = lax.axis_index("col")
    one, two, three = tables()
    blocks = x.reshape(16, 4, 256, C)
    place = jnp.stack([f, y, x_lo, jnp.int32(R3 + R2)])

    def for_partner(index, x_ref, out_ref):
        rows = rows_at(HALF * (1 - index[2]), HALF)
        return [(x_ref.at[:, g, rows, :], out_ref.at[g]) for g in range(4)]

    def for_self(index, x_ref, out_ref):
        rows = rows_at(HALF * index[2], HALF)
        return [(x_ref.at[:, g, rows, :], out_ref.at[g, 0]) for g in range(4)]

    def for_z(index, x_ref, out_ref):
        return [(x_ref.at[:, g, rows_at(index[3], R1), :], out_ref.at[g]) for g in range(4)]

    def for_y(r):
        def views(index, x_ref, out_ref):
            rows = rows_at(R3 + QUARTER * ((index[1] + r) % 4), QUARTER)
            return [(x_ref.at[:, :, rows, :], out_ref)]

        return pack(place, blocks, views, 1, (16, 4, QUARTER, C), (16, 4, QUARTER, C), 2)

    third_far = shift(pack(place, blocks, for_partner, 4, (16, HALF, C), (4, 16, HALF, C), 3), "x_lo")
    first = exchange(pack(place, blocks, for_z, 4, (16, R1, C), (4, 16, R1, C), 5), "z")
    second = [shift(for_y(r), "y", r) for r in (1, 2, 3)]
    third = pack(place, blocks, for_self, 4, (16, HALF, C), (4, 2, 16, HALF, C), 3)
    first, second, third, third_far = together(first, second, third, third_far)

    third = exchange(join(third, third_far), "z")
    slots = dft_by_owner(place, one, first, 9)
    slots, second = together(slots, second)
    mine1, other1 = reduce_ring(slots, "y")
    mine, other = dft_by_row(jnp.stack([4 * f + z, y]), two, blocks, second)
    own2 = mine + shift(other, "x_lo")
    mine1, other1, own2, third = together(mine1, other1, own2, third)

    own2 = jnp.sum(exchange(own2, "z"), axis=0)
    own1 = mine1 + shift(other1, "x_lo")
    below1, above1 = near_z(own1)
    far1 = shift(own1, "x_hi")
    mine3, other3 = reduce_ring(dft_by_owner(place, three, third.reshape(8, 16, HALF, C), 7), "y")
    own2 = exchange(own2.reshape(4, 8, QUARTER, C), "y")
    own2 = jnp.transpose(own2, (1, 0, 2, 3)).reshape(8, R2, C)
    own1, below1, above1, far1, own2, mine3, other3 = together(own1, below1, above1, far1, own2, mine3, other3)

    other3 = shift(other3, "x_lo")
    below2, above2 = near_z(own2)
    across1 = across_z(below1, above1)
    far2 = shift(own2, "x_hi")
    own3 = jnp.where(x_lo == 0, jnp.concatenate([mine3, other3], axis=1), jnp.concatenate([other3, mine3], axis=1))
    own3, below2, above2, across1, far2 = together(own3, below2, above2, across1, far2)

    below3, above3 = near_z(own3)
    across2 = across_z(below2, above2)
    far3 = shift(own3, "x_hi")
    across3 = across_z(below3, above3)

    def columns(own, far):
        return [own, shift(own, "core"), far, shift(far, "core")]

    left = [columns(own3, far3), columns(own2, far2), columns(own1, far1)]
    right = [(own3, above3, below3), (own2, above2, below2), (own1, above1, below1)]
    return product(jnp.stack([col, z]), left, right, [across3, across2, across1], (0, R3, R3 + R2))


def solution(mesh):
    in_specs = (P(("freq", "row"), None, "col"),)
    out_specs = P(None, "freq", "row", "col")
    return jax.shard_map(local, mesh=mesh, in_specs=in_specs, out_specs=out_specs, check_vma=False)
```

```python
import functools
import math

import jax
import jax.numpy as jnp
import numpy as np
from jax import lax
from jax.experimental import pallas as pl
from jax.experimental.pallas import tpu as pltpu
from jax.sharding import PartitionSpec as P

S = 1024
NT = 512
NF = 32
C = 256
R3, R2, R1 = 96, 64, 96
HALF, QUARTER = R3 // 2, R2 // 4
VMEM = 50 << 20


def shift(x, axis, by=1):
    if axis == "z":
        return lax.ppermute(x, "row", [(i, (i + by) % 4) for i in range(4)])
    if axis == "y":
        return lax.ppermute(x, "freq", [(i, (i + 2 * by) % 8) for i in range(8)])
    if axis == "x_lo":
        return lax.ppermute(x, "freq", [(i, i ^ 1) for i in range(8)])
    if axis == "x_hi":
        return lax.ppermute(x, "col", [(i, i ^ 2) for i in range(4)])
    return lax.ppermute(x, "col", [(i, i ^ 1) for i in range(4)])


def exchange(x, axis):
    if axis == "z":
        return lax.all_to_all(x, "row", split_axis=0, concat_axis=0, tiled=True)
    groups = [[2 * j + i for j in range(4)] for i in range(2)]
    return lax.all_to_all(x, "freq", split_axis=0, concat_axis=0, tiled=True, axis_index_groups=groups)


def together(*values):
    return lax.optimization_barrier(values)


def cost(us):
    return pl.CostEstimate(flops=0, bytes_accessed=int(us * 3.6e6), transcendentals=0)


def call(kernel, index, operands, grid, in_specs, out_specs, out_shape, us, scratch_shapes=()):
    return pl.pallas_call(
        kernel,
        grid_spec=pltpu.PrefetchScalarGridSpec(
            num_scalar_prefetch=1, grid=grid, in_specs=in_specs, out_specs=out_specs, scratch_shapes=scratch_shapes
        ),
        out_shape=out_shape,
        compiler_params=pltpu.CompilerParams(vmem_limit_bytes=VMEM),
        cost_estimate=cost(us),
    )(index, *operands)


def f32(*shape):
    return jax.ShapeDtypeStruct(shape, jnp.float32)


def tables():
    k = np.arange(NF) + 1
    phase = np.outer(k, np.arange(NT)) % NT * (2.0 * math.pi / NT)
    scale = 1.0 / math.sqrt(NT * math.sqrt(S))
    full = np.stack([np.cos(phase), -np.sin(phase)]) * scale
    full = full.reshape(2, 8, 4, NT).transpose(1, 0, 2, 3).reshape(8, 8, NT).astype(np.float32)
    one, two, three = [], [], []
    u = np.arange(16)
    for f in range(8):
        y, x_lo = f // 2, f % 2
        by_y = [2 * ((y + ry) % 4) + (x_lo + q) % 2 for ry in range(4) for q in range(2)]
        by_q = [2 * y_to + (x_lo + q) % 2 for q in range(2) for y_to in range(4)]
        by_y, by_q = full[by_y].reshape(64, NT), full[by_q].reshape(64, NT)
        near, far = 64 * f + np.arange(64), 64 * (f ^ 1) + np.arange(64)
        one.append(by_y[:, near])
        three.append(by_y[:, np.stack([near.reshape(4, 16), far.reshape(4, 16)], axis=1).reshape(-1)])
        for z in range(4):
            t = [128 * ((y - r) % 4) + 64 * x_lo + 16 * z + u for r in range(4)]
            two.append(by_q[:, np.concatenate(t)])
    return np.stack(one), np.stack(two), np.stack(three)


def staged(pairs, stage_ref, in_sem, out_sem):
    ins = [pltpu.make_async_copy(a, stage_ref.at[n], in_sem.at[n]) for n, (a, _) in enumerate(pairs)]
    outs = [pltpu.make_async_copy(stage_ref.at[n], b, out_sem.at[n]) for n, (_, b) in enumerate(pairs)]
    for copy in ins:
        copy.start()
    for copy_in, copy_out in zip(ins, outs):
        copy_in.wait()
        copy_out.start()
    for copy in outs:
        copy.wait()


def pack_kernel(index, x_ref, out_ref, *scratch, views):
    staged(views(index, x_ref, out_ref), *scratch)


def stage(n, shape):
    return [pltpu.VMEM((n, *shape), jnp.float32), pltpu.SemaphoreType.DMA((n,)), pltpu.SemaphoreType.DMA((n,))]


def pack(index, blocks, views, n, piece, shape, us):
    anywhere = pl.BlockSpec(memory_space=pl.ANY)
    return call(
        functools.partial(pack_kernel, views=views),
        index,
        (blocks,),
        (1,),
        [anywhere],
        anywhere,
        f32(*shape),
        us,
        stage(n, piece),
    )


def join_kernel(far_ref, joined_ref, out_ref, *scratch):
    del joined_ref
    staged([(far_ref.at[g], out_ref.at[g, 1]) for g in range(4)], *scratch)


def join(joined, far):
    anywhere = pl.BlockSpec(memory_space=pl.ANY)
    return pl.pallas_call(
        join_kernel,
        in_specs=[anywhere] * 2,
        out_specs=anywhere,
        out_shape=f32(*joined.shape),
        scratch_shapes=stage(4, far.shape[1:]),
        input_output_aliases={1: 0},
        compiler_params=pltpu.CompilerParams(vmem_limit_bytes=VMEM),
        cost_estimate=cost(3),
    )(far, joined)


def rows_at(start, size):
    return pl.ds(pl.multiple_of(start, 8), size)


def transform(w_ref, samples, store, rows):
    w = w_ref[0]
    wh = w.astype(jnp.bfloat16)
    wl = (w - wh.astype(jnp.float32)).astype(jnp.bfloat16)
    wcat = jnp.concatenate([wh, wh, wl], axis=1)
    for s in range(rows):
        x = samples(s)
        xh = x.astype(jnp.bfloat16)
        xl = (x - xh.astype(jnp.float32)).astype(jnp.bfloat16)
        xcat = jnp.concatenate([xh, xl, xh], axis=0)
        store(s, jnp.dot(wcat, xcat, preferred_element_type=jnp.float32))


def dft_owner_kernel(rows, _, w_ref, x_ref, *outs):
    def samples(s):
        return jnp.concatenate([x_ref[j, :, s, :] for j in range(x_ref.shape[0])], axis=0)

    def store(s, res):
        for i, out in enumerate(outs):
            out[:, s, :] = res[8 * i : 8 * i + 8]

    transform(w_ref, samples, store, rows)


def dft_by_owner(index, w, x, us):
    n, _, rows, _ = x.shape
    block = 16
    flat = call(
        functools.partial(dft_owner_kernel, block),
        index,
        (w, x),
        (rows // block,),
        [
            pl.BlockSpec((1, 64, w.shape[2]), lambda g, i: (i[0], 0, 0)),
            pl.BlockSpec((n, 16, block, C), lambda g, i: (0, 0, g, 0)),
        ],
        [pl.BlockSpec((8, block, C), lambda g, i: (0, g, 0))] * 8,
        [f32(8, rows, C)] * 8,
        us,
    )
    return [flat[2 * r : 2 * r + 2] for r in range(4)]


def dft_row_kernel(rows, _, w_ref, *refs):
    pieces, outs = refs[:4], refs[4:]

    def samples(s):
        return jnp.concatenate([p[:, 0, s, :] for p in pieces], axis=0)

    def store(s, res):
        for q in range(2):
            outs[q][0, :, s, :] = res[32 * q : 32 * q + 32]

    transform(w_ref, samples, store, rows)


def dft_by_row(index, w, blocks, pieces):
    at = R3 // QUARTER
    return call(
        functools.partial(dft_row_kernel, QUARTER),
        index,
        (w, blocks, *pieces),
        (4,),
        [
            pl.BlockSpec((1, 64, 64), lambda g, i: (i[0], 0, 0)),
            pl.BlockSpec((16, 1, QUARTER, C), lambda g, i: (0, g, at + i[1], 0)),
        ]
        + [pl.BlockSpec((16, 1, QUARTER, C), lambda g, i: (0, g, 0, 0))] * 3,
        [pl.BlockSpec((1, 32, QUARTER, C), lambda g, i: (g, 0, 0, 0))] * 2,
        [f32(4, 32, QUARTER, C)] * 2,
        7,
    )


def reduce_ring(slots, axis):
    up0 = shift(slots[2][0], axis, 1)
    down1 = shift(slots[2][1], axis, -1)
    up1 = shift(slots[1][1], axis, 1)
    down0 = shift(slots[3][0], axis, -1)
    up0 = shift(slots[1][0] + up0, axis, 1)
    down1 = shift(slots[3][1] + down1, axis, -1)
    return [slots[0][0] + up0 + down0, slots[0][1] + up1 + down1]


def near_z(x):
    return shift(x, "z", 1), shift(x, "z", -1)


def across_z(below, above):
    return shift(below[:4], "z", 1), shift(above[4:], "z", -1)


def split(x):
    hi = x.astype(jnp.bfloat16)
    return hi, (x - hi.astype(jnp.float32)).astype(jnp.bfloat16)


def dots(a, b, out, total):
    def dot(x, y):
        return jnp.dot(x, y, preferred_element_type=jnp.float32)

    rr, ri = total
    ii, ir = jnp.zeros((256, C), jnp.float32), jnp.zeros((256, C), jnp.float32)
    for (arh, arl, aih, ail), (brh, brl, bih, bil) in zip(a, b):
        rr += dot(arh, brh) + dot(arh, brl) + dot(arl, brh)
        ii += dot(aih, bih) + dot(aih, bil) + dot(ail, bih)
        ri += dot(arh, bih) + dot(arh, bil) + dot(arl, bih)
        ir += dot(aih, brh) + dot(aih, brl) + dot(ail, brh)
    out[0, 0] = rr - ii
    out[1, 0] = ri + ir


def near_kernel(left_rows, right_rows, index, *refs):
    n, m = 8 * len(left_rows), 6 * len(right_rows)
    left, right = refs[:n], refs[n : n + m]
    out, kept, a_ref, b_ref = refs[n + m :]
    col, z = index[0], index[1]
    for part in range(2):
        for i, rows in enumerate(left_rows):
            for e in range(4):
                hi, lo = split(left[8 * i + 2 * e + part][0])
                a_ref[col ^ e, 2 * part, rows] = hi
                a_ref[col ^ e, 2 * part + 1, rows] = lo
        for i, rows in enumerate(right_rows):
            for t in range(3):
                hi, lo = split(right[6 * i + 2 * t + part][0])
                b_ref[t, 2 * part, rows] = hi
                b_ref[t, 2 * part + 1, rows] = lo
    zero = jnp.zeros((256, C), jnp.float32)
    a = [[a_ref[(z + r) % 4, j] for j in range(4)] for r in (0, 1, 3)]
    dots(a, [[b_ref[t, j] for j in range(4)] for t in range(3)], out, (zero, zero))
    kept[0] = a_ref[(z + 2) % 4]


def far_kernel(right_rows, _, total, kept, *refs):
    out, b_ref = refs[-2:]
    for i, rows in enumerate(right_rows):
        for part in range(2):
            hi, lo = split(refs[2 * i + part][0])
            b_ref[2 * part, rows] = hi
            b_ref[2 * part + 1, rows] = lo
    a, b = [kept[0, j] for j in range(4)], [b_ref[j] for j in range(4)]
    dots([a], [b], out, (total[0, 0], total[1, 0]))


def product(index, left, right, across, left_starts, right_starts):
    def segments(parts, starts):
        return [slice(a, a + part[0].shape[1]) for a, part in zip(starts, parts)]

    left_rows, right_rows = segments(left, left_starts), segments(right, right_starts)
    sizes = [part[0].shape[1] for part in right]

    def spec(rows, first):
        return pl.BlockSpec((1, rows, C), lambda g, _: (first + g, 0, 0))

    def both(groups):
        operands, specs = [], []
        for arrays in groups:
            for array in arrays:
                operands += [array, array]
                specs += [spec(array.shape[1], 0), spec(array.shape[1], 4)]
        return operands, specs

    left, left_specs = both(left)
    right, right_specs = both(right)
    out_spec = pl.BlockSpec((2, 1, 256, C), lambda g, _: (0, g, 0, 0))
    kept_spec = pl.BlockSpec((1, 4, 256, C), lambda g, _: (g, 0, 0, 0))
    total, kept = call(
        functools.partial(near_kernel, left_rows, right_rows),
        index,
        left + right,
        (4,),
        left_specs + right_specs,
        [out_spec, kept_spec],
        [f32(2, 4, 256, C), jax.ShapeDtypeStruct((4, 4, 256, C), jnp.bfloat16)],
        11,
        [pltpu.VMEM((4, 4, 256, C), jnp.bfloat16), pltpu.VMEM((3, 4, 256, C), jnp.bfloat16)],
    )
    return call(
        functools.partial(far_kernel, right_rows),
        index,
        [total, kept] + [array for pair in across for array in pair],
        (4,),
        [out_spec, kept_spec] + [spec(rows, 0) for rows in sizes for _ in range(2)],
        out_spec,
        f32(2, 4, 256, C),
        4,
        [pltpu.VMEM((4, 256, C), jnp.bfloat16)],
    )


def local(x):
    f = lax.axis_index("freq")
    y, x_lo = f // 2, f % 2
    z = lax.axis_index("row")
    col = lax.axis_index("col")
    one, two, three = tables()
    blocks = x.reshape(16, 4, 256, C)
    place = jnp.stack([f, y, x_lo, jnp.int32(R3 + R2)])

    def for_partner(index, x_ref, out_ref):
        rows = rows_at(HALF * (1 - index[2]), HALF)
        return [(x_ref.at[:, g, rows, :], out_ref.at[g]) for g in range(4)]

    def for_self(index, x_ref, out_ref):
        rows = rows_at(HALF * index[2], HALF)
        return [(x_ref.at[:, g, rows, :], out_ref.at[g, 0]) for g in range(4)]

    def for_z(index, x_ref, out_ref):
        return [(x_ref.at[:, g, rows_at(index[3], R1), :], out_ref.at[g]) for g in range(4)]

    def for_y(r):
        def views(index, x_ref, out_ref):
            rows = rows_at(R3 + QUARTER * ((index[1] + r) % 4), QUARTER)
            return [(x_ref.at[:, :, rows, :], out_ref)]

        return pack(place, blocks, views, 1, (16, 4, QUARTER, C), (16, 4, QUARTER, C), 2)

    third_far = shift(pack(place, blocks, for_partner, 4, (16, HALF, C), (4, 16, HALF, C), 3), "x_lo")
    first = exchange(pack(place, blocks, for_z, 4, (16, R1, C), (4, 16, R1, C), 5), "z")
    second = [shift(for_y(r), "y", r) for r in (1, 2, 3)]
    third = pack(place, blocks, for_self, 4, (16, HALF, C), (4, 2, 16, HALF, C), 3)
    second = dft_by_row(jnp.stack([4 * f + z, y]), two, blocks, second)
    first, second, third, third_far = together(first, second, third, third_far)

    third = exchange(join(third, third_far), "z")
    own2 = second[0] + shift(second[1], "x_lo")
    mine1, other1 = reduce_ring(dft_by_owner(place, one, first, 9), "y")
    mine1, other1, own2, third = together(mine1, other1, own2, third)

    own2 = jnp.sum(exchange(own2, "z"), axis=0)
    own1 = mine1 + shift(other1, "x_lo")
    below1, above1 = near_z(own1)
    far1 = shift(own1, "x_hi")
    mine3, other3 = reduce_ring(dft_by_owner(place, three, third.reshape(8, 16, HALF, C), 7), "y")
    own2 = exchange(own2.reshape(4, 8, QUARTER, C), "y")
    own2 = jnp.transpose(own2, (1, 0, 2, 3)).reshape(8, R2, C)
    across1 = across_z(below1, above1)
    below2, above2 = near_z(own2)
    mine3, other3 = together(mine3, other3)

    other3 = shift(other3, "x_lo")
    own3 = jnp.where(x_lo == 0, jnp.concatenate([mine3, other3], axis=1), jnp.concatenate([other3, mine3], axis=1))
    far2 = shift(own2, "x_hi")
    own3, below2, above2, across1 = together(own3, below2, above2, across1)

    below3, above3 = near_z(own3)
    across2 = across_z(below2, above2)
    far3 = shift(own3, "x_hi")
    below3, above3, far2, far3, across2 = together(below3, above3, far2, far3, across2)
    across3 = across_z(below3, above3)

    left = [[own, shift(own, "core"), far, shift(far, "core")] for own, far in ((own3, far3), (own2, far2), (own1, far1))]
    right = [(own3, above3, below3), (own2, above2, below2), (own1, above1, below1)]
    starts = (0, R3, R3 + R2)
    return product(jnp.stack([col, z]), left, right, [across3, across2, across1], starts, starts)


def solution(mesh):
    in_specs = (P(("freq", "row"), None, "col"),)
    out_specs = P(None, "freq", "row", "col")
    return jax.shard_map(local, mesh=mesh, in_specs=in_specs, out_specs=out_specs, check_vma=False)
```

```python
import functools
import math

import jax
import jax.numpy as jnp
import numpy as np
from jax import lax
from jax.experimental import pallas as pl
from jax.experimental.pallas import tpu as pltpu
from jax.sharding import PartitionSpec as P

S = 1024
NT = 512
NF = 32
C = 256
R3, R2, R1 = 96, 64, 96
HALF, QUARTER = R3 // 2, R2 // 4
VMEM = 50 << 20


def shift(x, axis, by=1):
    if axis == "z":
        return lax.ppermute(x, "row", [(i, (i + by) % 4) for i in range(4)])
    if axis == "y":
        return lax.ppermute(x, "freq", [(i, (i + 2 * by) % 8) for i in range(8)])
    if axis == "x_lo":
        return lax.ppermute(x, "freq", [(i, i ^ 1) for i in range(8)])
    if axis == "x_hi":
        return lax.ppermute(x, "col", [(i, i ^ 2) for i in range(4)])
    return lax.ppermute(x, "col", [(i, i ^ 1) for i in range(4)])


def exchange(x, axis):
    if axis == "z":
        return lax.all_to_all(x, "row", split_axis=0, concat_axis=0, tiled=True)
    groups = [[2 * j + i for j in range(4)] for i in range(2)]
    return lax.all_to_all(x, "freq", split_axis=0, concat_axis=0, tiled=True, axis_index_groups=groups)


def together(*values):
    return lax.optimization_barrier(values)


def cost(us):
    return pl.CostEstimate(flops=0, bytes_accessed=int(us * 3.6e6), transcendentals=0)


def call(kernel, index, operands, grid, in_specs, out_specs, out_shape, us, scratch_shapes=()):
    return pl.pallas_call(
        kernel,
        grid_spec=pltpu.PrefetchScalarGridSpec(
            num_scalar_prefetch=1, grid=grid, in_specs=in_specs, out_specs=out_specs, scratch_shapes=scratch_shapes
        ),
        out_shape=out_shape,
        compiler_params=pltpu.CompilerParams(vmem_limit_bytes=VMEM),
        cost_estimate=cost(us),
    )(index, *operands)


def f32(*shape):
    return jax.ShapeDtypeStruct(shape, jnp.float32)


def tables():
    k = np.arange(NF) + 1
    phase = np.outer(k, np.arange(NT)) % NT * (2.0 * math.pi / NT)
    scale = 1.0 / math.sqrt(NT * math.sqrt(S))
    full = np.stack([np.cos(phase), -np.sin(phase)]) * scale
    full = full.reshape(2, 8, 4, NT).transpose(1, 0, 2, 3).reshape(8, 8, NT).astype(np.float32)
    one, two, three = [], [], []
    u = np.arange(16)
    for f in range(8):
        y, x_lo = f // 2, f % 2
        by_y = [2 * ((y + ry) % 4) + (x_lo + q) % 2 for ry in range(4) for q in range(2)]
        by_q = [2 * y_to + (x_lo + q) % 2 for q in range(2) for y_to in range(4)]
        by_y, by_q = full[by_y].reshape(64, NT), full[by_q].reshape(64, NT)
        near, far = 64 * f + np.arange(64), 64 * (f ^ 1) + np.arange(64)
        one.append(by_y[:, near])
        three.append(by_y[:, np.stack([near.reshape(4, 16), far.reshape(4, 16)], axis=1).reshape(-1)])
        for z in range(4):
            t = [128 * ((y - r) % 4) + 64 * x_lo + 16 * z + u for r in range(4)]
            two.append(by_q[:, np.concatenate(t)])
    return np.stack(one), np.stack(two), np.stack(three)


def staged(pairs, stage_ref, in_sem, out_sem):
    ins = [pltpu.make_async_copy(a, stage_ref.at[n], in_sem.at[n]) for n, (a, _) in enumerate(pairs)]
    outs = [pltpu.make_async_copy(stage_ref.at[n], b, out_sem.at[n]) for n, (_, b) in enumerate(pairs)]
    for copy in ins:
        copy.start()
    for copy_in, copy_out in zip(ins, outs):
        copy_in.wait()
        copy_out.start()
    for copy in outs:
        copy.wait()


def pack_kernel(index, x_ref, out_ref, *scratch, views):
    staged(views(index, x_ref, out_ref), *scratch)


def stage(n, shape):
    return [pltpu.VMEM((n, *shape), jnp.float32), pltpu.SemaphoreType.DMA((n,)), pltpu.SemaphoreType.DMA((n,))]


def pack(index, blocks, views, n, piece, shape, us):
    anywhere = pl.BlockSpec(memory_space=pl.ANY)
    return call(
        functools.partial(pack_kernel, views=views),
        index,
        (blocks,),
        (1,),
        [anywhere],
        anywhere,
        f32(*shape),
        us,
        stage(n, piece),
    )


def join_kernel(far_ref, joined_ref, out_ref, *scratch):
    del joined_ref
    staged([(far_ref.at[g], out_ref.at[g, 1]) for g in range(4)], *scratch)


def join(joined, far):
    anywhere = pl.BlockSpec(memory_space=pl.ANY)
    return pl.pallas_call(
        join_kernel,
        in_specs=[anywhere] * 2,
        out_specs=anywhere,
        out_shape=f32(*joined.shape),
        scratch_shapes=stage(4, far.shape[1:]),
        input_output_aliases={1: 0},
        compiler_params=pltpu.CompilerParams(vmem_limit_bytes=VMEM),
        cost_estimate=cost(3),
    )(far, joined)


def rows_at(start, size):
    return pl.ds(pl.multiple_of(start, 8), size)


def transform(w_ref, samples, store, rows):
    w = w_ref[0]
    wh = w.astype(jnp.bfloat16)
    wl = (w - wh.astype(jnp.float32)).astype(jnp.bfloat16)
    wcat = jnp.concatenate([wh, wh, wl], axis=1)
    for s in range(rows):
        x = samples(s)
        xh = x.astype(jnp.bfloat16)
        xl = (x - xh.astype(jnp.float32)).astype(jnp.bfloat16)
        xcat = jnp.concatenate([xh, xl, xh], axis=0)
        store(s, jnp.dot(wcat, xcat, preferred_element_type=jnp.float32))


def dft_owner_kernel(rows, _, w_ref, x_ref, *outs):
    def samples(s):
        return jnp.concatenate([x_ref[j, :, s, :] for j in range(x_ref.shape[0])], axis=0)

    def store(s, res):
        for i, out in enumerate(outs):
            out[:, s, :] = res[8 * i : 8 * i + 8]

    transform(w_ref, samples, store, rows)


def dft_by_owner(index, w, x, us):
    n, _, rows, _ = x.shape
    block = {96: 32, 48: 24}[rows]
    flat = call(
        functools.partial(dft_owner_kernel, block),
        index,
        (w, x),
        (rows // block,),
        [
            pl.BlockSpec((1, 64, w.shape[2]), lambda g, i: (i[0], 0, 0)),
            pl.BlockSpec((n, 16, block, C), lambda g, i: (0, 0, g, 0)),
        ],
        [pl.BlockSpec((8, block, C), lambda g, i: (0, g, 0))] * 8,
        [f32(8, rows, C)] * 8,
        us,
    )
    return [flat[2 * r : 2 * r + 2] for r in range(4)]


def dft_row_kernel(rows, _, w_ref, *refs):
    pieces, outs = refs[:4], refs[4:]

    def samples(s):
        return jnp.concatenate([p[:, 0, s, :] for p in pieces], axis=0)

    def store(s, res):
        for q in range(2):
            outs[q][0, :, s, :] = res[32 * q : 32 * q + 32]

    transform(w_ref, samples, store, rows)


def dft_by_row(index, w, blocks, pieces):
    at = R3 // QUARTER
    return call(
        functools.partial(dft_row_kernel, QUARTER),
        index,
        (w, blocks, *pieces),
        (4,),
        [
            pl.BlockSpec((1, 64, 64), lambda g, i: (i[0], 0, 0)),
            pl.BlockSpec((16, 1, QUARTER, C), lambda g, i: (0, g, at + i[1], 0)),
        ]
        + [pl.BlockSpec((16, 1, QUARTER, C), lambda g, i: (0, g, 0, 0))] * 3,
        [pl.BlockSpec((1, 32, QUARTER, C), lambda g, i: (g, 0, 0, 0))] * 2,
        [f32(4, 32, QUARTER, C)] * 2,
        7,
    )


def reduce_ring(slots, axis):
    up0 = shift(slots[2][0], axis, 1)
    down1 = shift(slots[2][1], axis, -1)
    up1 = shift(slots[1][1], axis, 1)
    down0 = shift(slots[3][0], axis, -1)
    up0 = shift(slots[1][0] + up0, axis, 1)
    down1 = shift(slots[3][1] + down1, axis, -1)
    return [slots[0][0] + up0 + down0, slots[0][1] + up1 + down1]


def near_z(x):
    return shift(x, "z", 1), shift(x, "z", -1)


def across_z(below, above):
    return shift(below[:4], "z", 1), shift(above[4:], "z", -1)


def split(x):
    hi = x.astype(jnp.bfloat16)
    return hi, (x - hi.astype(jnp.float32)).astype(jnp.bfloat16)


def store_left(a_ref, block, rows, real, imag):
    for part, x in enumerate((real, imag, real + imag)):
        hi, lo = split(x)
        a_ref[block, part, rows, 0:256] = hi
        a_ref[block, part, rows, 256:512] = hi
        a_ref[block, part, rows, 512:768] = lo


def store_right(b_ref, block, rows, real, imag):
    for part, x in enumerate((real, imag, real + imag)):
        hi, lo = split(x)
        b_ref[block, part, rows] = hi
        b_ref[block, part, slice(256 + rows.start, 256 + rows.stop)] = lo
        b_ref[block, part, slice(512 + rows.start, 512 + rows.stop)] = hi


def dots(pairs, out, real, imag):
    def dot(x, y):
        return jnp.dot(x, y, preferred_element_type=jnp.float32)

    for a, b in pairs:
        rr, ii, both = (dot(a[part], b[part]) for part in range(3))
        real = real + (rr - ii)
        imag = imag + (both - rr - ii)
    out[0, 0] = real
    out[1, 0] = imag


def near_kernel(left_rows, right_rows, index, *refs):
    n, m = 4 * len(left_rows), 3 * len(right_rows)
    left, right = refs[:n], refs[n : n + m]
    out, kept, a_ref, b_ref = refs[n + m :]
    col, z = index[0], index[1]
    for i, rows in enumerate(left_rows):
        for e in range(4):
            x = left[4 * i + e]
            store_left(a_ref, col ^ e, rows, x[0, 0], x[1, 0])

            @pl.when((col ^ e) == (z + 2) % 4)
            def _(x=x, rows=rows):
                kept[:, 0, rows] = x[:, 0]

    for i, rows in enumerate(right_rows):
        for t in range(3):
            x = right[3 * i + t]
            store_right(b_ref, t, rows, x[0, 0], x[1, 0])
    pairs = []
    for t, r in enumerate((0, 1, 3)):
        k = (z + r) % 4
        pairs.append(([a_ref[k, part] for part in range(3)], [b_ref[t, part] for part in range(3)]))
    dots(pairs, out, 0.0, 0.0)


def far_kernel(right_rows, _, total, kept, *refs):
    out, a_ref, b_ref = refs[-3:]
    store_left(a_ref, 0, slice(0, 256), kept[0, 0], kept[1, 0])
    for i, rows in enumerate(right_rows):
        store_right(b_ref, 0, rows, refs[2 * i][0], refs[2 * i + 1][0])
    pair = ([a_ref[0, part] for part in range(3)], [b_ref[0, part] for part in range(3)])
    dots([pair], out, total[0, 0], total[1, 0])


def product(index, left, right, across, left_starts, right_starts):
    def segments(parts, starts):
        return [slice(a, a + part[0].shape[1]) for a, part in zip(starts, parts)]

    left_rows, right_rows = segments(left, left_starts), segments(right, right_starts)
    sizes = [part[0].shape[1] for part in right]

    def spec(rows):
        return pl.BlockSpec((1, rows, C), lambda g, _: (g, 0, 0))

    def both(groups):
        operands, specs = [], []
        for arrays in groups:
            for array in arrays:
                rows = array.shape[1]
                operands.append(array.reshape(2, 4, rows, C))
                specs.append(pl.BlockSpec((2, 1, rows, C), lambda g, _: (0, g, 0, 0)))
        return operands, specs

    left, left_specs = both(left)
    right, right_specs = both(right)
    out_spec = pl.BlockSpec((2, 1, 256, C), lambda g, _: (0, g, 0, 0))
    total, kept = call(
        functools.partial(near_kernel, left_rows, right_rows),
        index,
        left + right,
        (4,),
        left_specs + right_specs,
        [out_spec, out_spec],
        [f32(2, 4, 256, C)] * 2,
        11,
        [pltpu.VMEM((4, 3, 256, 768), jnp.bfloat16), pltpu.VMEM((3, 3, 768, C), jnp.bfloat16)],
    )
    return call(
        functools.partial(far_kernel, right_rows),
        index,
        [total, kept] + [array for pair in across for array in pair],
        (4,),
        [out_spec, out_spec] + [spec(rows) for rows in sizes for _ in range(2)],
        out_spec,
        f32(2, 4, 256, C),
        4,
        [pltpu.VMEM((1, 3, 256, 768), jnp.bfloat16), pltpu.VMEM((1, 3, 768, C), jnp.bfloat16)],
    )


def local(x):
    f = lax.axis_index("freq")
    y, x_lo = f // 2, f % 2
    z = lax.axis_index("row")
    col = lax.axis_index("col")
    one, two, three = tables()
    blocks = x.reshape(16, 4, 256, C)
    place = jnp.stack([f, y, x_lo, jnp.int32(R3 + R2)])

    def for_partner(index, x_ref, out_ref):
        rows = rows_at(HALF * (1 - index[2]), HALF)
        return [(x_ref.at[:, g, rows, :], out_ref.at[g]) for g in range(4)]

    def for_self(index, x_ref, out_ref):
        rows = rows_at(HALF * index[2], HALF)
        return [(x_ref.at[:, g, rows, :], out_ref.at[g, 0]) for g in range(4)]

    def for_z(index, x_ref, out_ref):
        return [(x_ref.at[:, g, rows_at(index[3], R1), :], out_ref.at[g]) for g in range(4)]

    def for_y(r):
        def views(index, x_ref, out_ref):
            rows = rows_at(R3 + QUARTER * ((index[1] + r) % 4), QUARTER)
            return [(x_ref.at[:, :, rows, :], out_ref)]

        return pack(place, blocks, views, 1, (16, 4, QUARTER, C), (16, 4, QUARTER, C), 2)

    third_far = shift(pack(place, blocks, for_partner, 4, (16, HALF, C), (4, 16, HALF, C), 3), "x_lo")
    first = exchange(pack(place, blocks, for_z, 4, (16, R1, C), (4, 16, R1, C), 5), "z")
    second = [shift(for_y(r), "y", r) for r in (1, 2, 3)]
    third = pack(place, blocks, for_self, 4, (16, HALF, C), (4, 2, 16, HALF, C), 3)
    second = dft_by_row(jnp.stack([4 * f + z, y]), two, blocks, second)
    first, second, third, third_far = together(first, second, third, third_far)

    third = exchange(join(third, third_far), "z")
    own2 = second[0] + shift(second[1], "x_lo")
    mine1, other1 = reduce_ring(dft_by_owner(place, one, first, 9), "y")
    mine1, other1, own2, third = together(mine1, other1, own2, third)

    own2 = jnp.sum(exchange(own2, "z"), axis=0)
    own1 = mine1 + shift(other1, "x_lo")
    below1, above1 = near_z(own1)
    far1 = shift(own1, "x_hi")
    mine3, other3 = reduce_ring(dft_by_owner(place, three, third.reshape(8, 16, HALF, C), 7), "y")
    own2 = exchange(own2.reshape(4, 8, QUARTER, C), "y")
    own2 = jnp.transpose(own2, (1, 0, 2, 3)).reshape(8, R2, C)
    across1 = across_z(below1, above1)
    below2, above2 = near_z(own2)
    mine3, other3, far1 = together(mine3, other3, far1)

    other3 = shift(other3, "x_lo")
    own3 = jnp.where(x_lo == 0, jnp.concatenate([mine3, other3], axis=1), jnp.concatenate([other3, mine3], axis=1))
    far2 = shift(own2, "x_hi")
    own3, below2, above2, across1 = together(own3, below2, above2, across1)

    below3, above3 = near_z(own3)
    across2 = across_z(below2, above2)
    far3 = shift(own3, "x_hi")
    below3, above3, far2, far3, across2 = together(below3, above3, far2, far3, across2)
    across3 = across_z(below3, above3)

    left = [[own, shift(own, "core"), far, shift(far, "core")] for own, far in ((own3, far3), (own2, far2), (own1, far1))]
    right = [(own3, above3, below3), (own2, above2, below2), (own1, above1, below1)]
    starts = (0, R3, R3 + R2)
    return product(jnp.stack([col, z]), left, right, [across3, across2, across1], starts, starts)


def solution(mesh):
    in_specs = (P(("freq", "row"), None, "col"),)
    out_specs = P(None, "freq", "row", "col")
    return jax.shard_map(local, mesh=mesh, in_specs=in_specs, out_specs=out_specs, check_vma=False)
```

```python
import functools
import math

import jax
import jax.numpy as jnp
import numpy as np
from jax import lax
from jax.experimental import pallas as pl
from jax.experimental.pallas import tpu as pltpu
from jax.sharding import PartitionSpec as P

S = 1024
NT = 512
NF = 32
C = 256
R3, R2, R1 = 96, 64, 96
HALF, QUARTER = R3 // 2, R2 // 4
VMEM = 50 << 20


def shift(x, axis, by=1):
    if axis == "z":
        return lax.ppermute(x, "row", [(i, (i + by) % 4) for i in range(4)])
    if axis == "y":
        return lax.ppermute(x, "freq", [(i, (i + 2 * by) % 8) for i in range(8)])
    if axis == "x_lo":
        return lax.ppermute(x, "freq", [(i, i ^ 1) for i in range(8)])
    if axis == "x_hi":
        return lax.ppermute(x, "col", [(i, i ^ 2) for i in range(4)])
    return lax.ppermute(x, "col", [(i, i ^ 1) for i in range(4)])


def exchange(x, axis):
    if axis == "z":
        return lax.all_to_all(x, "row", split_axis=0, concat_axis=0, tiled=True)
    groups = [[2 * j + i for j in range(4)] for i in range(2)]
    return lax.all_to_all(x, "freq", split_axis=0, concat_axis=0, tiled=True, axis_index_groups=groups)


def together(*values):
    return lax.optimization_barrier(values)


def cost(us):
    return pl.CostEstimate(flops=0, bytes_accessed=int(us * 3.6e6), transcendentals=0)


def call(kernel, index, operands, grid, in_specs, out_specs, out_shape, us, scratch_shapes=()):
    return pl.pallas_call(
        kernel,
        grid_spec=pltpu.PrefetchScalarGridSpec(
            num_scalar_prefetch=1, grid=grid, in_specs=in_specs, out_specs=out_specs, scratch_shapes=scratch_shapes
        ),
        out_shape=out_shape,
        compiler_params=pltpu.CompilerParams(vmem_limit_bytes=VMEM),
        cost_estimate=cost(us),
    )(index, *operands)


def f32(*shape):
    return jax.ShapeDtypeStruct(shape, jnp.float32)


def tables():
    k = np.arange(NF) + 1
    phase = np.outer(k, np.arange(NT)) % NT * (2.0 * math.pi / NT)
    scale = 1.0 / math.sqrt(NT * math.sqrt(S))
    full = np.stack([np.cos(phase), -np.sin(phase)]) * scale
    full = full.reshape(2, 8, 4, NT).transpose(1, 0, 2, 3).reshape(8, 8, NT).astype(np.float32)
    one, two, three = [], [], []
    u = np.arange(16)
    for f in range(8):
        y, x_lo = f // 2, f % 2
        by_y = [2 * ((y + ry) % 4) + (x_lo + q) % 2 for ry in range(4) for q in range(2)]
        by_q = [2 * y_to + (x_lo + q) % 2 for q in range(2) for y_to in range(4)]
        by_y, by_q = full[by_y].reshape(64, NT), full[by_q].reshape(64, NT)
        near, far = 64 * f + np.arange(64), 64 * (f ^ 1) + np.arange(64)
        one.append(by_y[:, near])
        three.append(by_y[:, np.stack([near.reshape(4, 16), far.reshape(4, 16)], axis=1).reshape(-1)])
        for z in range(4):
            t = [128 * ((y - r) % 4) + 64 * x_lo + 16 * z + u for r in range(4)]
            two.append(by_q[:, np.concatenate(t)])
    return np.stack(one), np.stack(two), np.stack(three)


def staged(pairs, stage_ref, in_sem, out_sem):
    ins = [pltpu.make_async_copy(a, stage_ref.at[n], in_sem.at[n]) for n, (a, _) in enumerate(pairs)]
    outs = [pltpu.make_async_copy(stage_ref.at[n], b, out_sem.at[n]) for n, (_, b) in enumerate(pairs)]
    for copy in ins:
        copy.start()
    for copy_in, copy_out in zip(ins, outs):
        copy_in.wait()
        copy_out.start()
    for copy in outs:
        copy.wait()


def pack_kernel(index, x_ref, out_ref, *scratch, views):
    staged(views(index, x_ref, out_ref), *scratch)


def stage(n, shape):
    return [pltpu.VMEM((n, *shape), jnp.float32), pltpu.SemaphoreType.DMA((n,)), pltpu.SemaphoreType.DMA((n,))]


def pack(index, blocks, views, n, piece, shape, us):
    anywhere = pl.BlockSpec(memory_space=pl.ANY)
    return call(
        functools.partial(pack_kernel, views=views),
        index,
        (blocks,),
        (1,),
        [anywhere],
        anywhere,
        f32(*shape),
        us,
        stage(n, piece),
    )


def join_kernel(far_ref, joined_ref, out_ref, *scratch):
    del joined_ref
    staged([(far_ref.at[g], out_ref.at[g, 1]) for g in range(4)], *scratch)


def join(joined, far):
    anywhere = pl.BlockSpec(memory_space=pl.ANY)
    return pl.pallas_call(
        join_kernel,
        in_specs=[anywhere] * 2,
        out_specs=anywhere,
        out_shape=f32(*joined.shape),
        scratch_shapes=stage(4, far.shape[1:]),
        input_output_aliases={1: 0},
        compiler_params=pltpu.CompilerParams(vmem_limit_bytes=VMEM),
        cost_estimate=cost(3),
    )(far, joined)


def rows_at(start, size):
    return pl.ds(pl.multiple_of(start, 8), size)


def transform(w_ref, samples, store, rows):
    w = w_ref[0]
    wh = w.astype(jnp.bfloat16)
    wl = (w - wh.astype(jnp.float32)).astype(jnp.bfloat16)
    both = jnp.concatenate([wh, wl], axis=0)
    for s in range(rows):
        x = samples(s)
        xh = x.astype(jnp.bfloat16)
        xl = (x - xh.astype(jnp.float32)).astype(jnp.bfloat16)
        high = jnp.dot(both, xh, preferred_element_type=jnp.float32)
        low = jnp.dot(wh, xl, preferred_element_type=jnp.float32)
        store(s, high[:64] + (high[64:] + low))


def dft_owner_kernel(rows, _, w_ref, x_ref, *outs):
    def samples(s):
        return jnp.concatenate([x_ref[j, :, s, :] for j in range(x_ref.shape[0])], axis=0)

    def store(s, res):
        for i, out in enumerate(outs):
            out[:, s, :] = res[8 * i : 8 * i + 8]

    transform(w_ref, samples, store, rows)


def dft_by_owner(index, w, x, us):
    n, _, rows, _ = x.shape
    block = {96: 32, 48: 24}[rows]
    flat = call(
        functools.partial(dft_owner_kernel, block),
        index,
        (w, x),
        (rows // block,),
        [
            pl.BlockSpec((1, 64, w.shape[2]), lambda g, i: (i[0], 0, 0)),
            pl.BlockSpec((n, 16, block, C), lambda g, i: (0, 0, g, 0)),
        ],
        [pl.BlockSpec((8, block, C), lambda g, i: (0, g, 0))] * 8,
        [f32(8, rows, C)] * 8,
        us,
    )
    return [flat[2 * r : 2 * r + 2] for r in range(4)]


def dft_row_kernel(rows, _, w_ref, *refs):
    pieces, outs = refs[:4], refs[4:]

    def samples(s):
        return jnp.concatenate([p[:, 0, s, :] for p in pieces], axis=0)

    def store(s, res):
        for q in range(2):
            outs[q][0, :, s, :] = res[32 * q : 32 * q + 32]

    transform(w_ref, samples, store, rows)


def dft_by_row(index, w, blocks, pieces):
    at = R3 // QUARTER
    return call(
        functools.partial(dft_row_kernel, QUARTER),
        index,
        (w, blocks, *pieces),
        (4,),
        [
            pl.BlockSpec((1, 64, 64), lambda g, i: (i[0], 0, 0)),
            pl.BlockSpec((16, 1, QUARTER, C), lambda g, i: (0, g, at + i[1], 0)),
        ]
        + [pl.BlockSpec((16, 1, QUARTER, C), lambda g, i: (0, g, 0, 0))] * 3,
        [pl.BlockSpec((1, 32, QUARTER, C), lambda g, i: (g, 0, 0, 0))] * 2,
        [f32(4, 32, QUARTER, C)] * 2,
        7,
    )


def reduce_ring(slots, axis):
    up0 = shift(slots[2][0], axis, 1)
    down1 = shift(slots[2][1], axis, -1)
    up1 = shift(slots[1][1], axis, 1)
    down0 = shift(slots[3][0], axis, -1)
    up0 = shift(slots[1][0] + up0, axis, 1)
    down1 = shift(slots[3][1] + down1, axis, -1)
    return [slots[0][0] + up0 + down0, slots[0][1] + up1 + down1]


def near_z(x):
    return shift(x, "z", 1), shift(x, "z", -1)


def across_z(below, above):
    return shift(below[:4], "z", 1), shift(above[4:], "z", -1)


def split(x):
    hi = x.astype(jnp.bfloat16)
    return hi, (x - hi.astype(jnp.float32)).astype(jnp.bfloat16)


def store_left(a_ref, block, rows, real, imag):
    for part, x in enumerate((real, imag, real + imag)):
        hi, lo = split(x)
        a_ref[block, part, rows, 0:256] = hi
        a_ref[block, part, rows, 256:512] = hi
        a_ref[block, part, rows, 512:768] = lo


def store_right(b_ref, block, rows, real, imag):
    for part, x in enumerate((real, imag, real + imag)):
        hi, lo = split(x)
        b_ref[block, part, rows] = hi
        b_ref[block, part, slice(256 + rows.start, 256 + rows.stop)] = lo
        b_ref[block, part, slice(512 + rows.start, 512 + rows.stop)] = hi


def dots(pairs, out, real, imag):
    def dot(x, y):
        return jnp.dot(x, y, preferred_element_type=jnp.float32)

    for a, b in pairs:
        rr, ii, both = (dot(a[part], b[part]) for part in range(3))
        real = real + (rr - ii)
        imag = imag + (both - rr - ii)
    out[0, 0] = real
    out[1, 0] = imag


def near_kernel(left_rows, right_rows, index, *refs):
    n, m = 4 * len(left_rows), 3 * len(right_rows)
    left, right = refs[:n], refs[n : n + m]
    out, kept, a_ref, b_ref = refs[n + m :]
    col, z = index[0], index[1]
    for i, rows in enumerate(left_rows):
        for e in range(4):
            x = left[4 * i + e]
            store_left(a_ref, col ^ e, rows, x[0, 0], x[1, 0])

            @pl.when((col ^ e) == (z + 2) % 4)
            def _(x=x, rows=rows):
                kept[:, 0, rows] = x[:, 0]

    for i, rows in enumerate(right_rows):
        for t in range(3):
            x = right[3 * i + t]
            store_right(b_ref, t, rows, x[0, 0], x[1, 0])
    pairs = []
    for t, r in enumerate((0, 1, 3)):
        k = (z + r) % 4
        pairs.append(([a_ref[k, part] for part in range(3)], [b_ref[t, part] for part in range(3)]))
    dots(pairs, out, 0.0, 0.0)


def far_kernel(right_rows, _, total, kept, *refs):
    out, a_ref, b_ref = refs[-3:]
    store_left(a_ref, 0, slice(0, 256), kept[0, 0], kept[1, 0])
    for i, rows in enumerate(right_rows):
        store_right(b_ref, 0, rows, refs[2 * i][0], refs[2 * i + 1][0])
    pair = ([a_ref[0, part] for part in range(3)], [b_ref[0, part] for part in range(3)])
    dots([pair], out, total[0, 0], total[1, 0])


def product(index, left, right, across, left_starts, right_starts):
    def segments(parts, starts):
        return [slice(a, a + part[0].shape[1]) for a, part in zip(starts, parts)]

    left_rows, right_rows = segments(left, left_starts), segments(right, right_starts)
    sizes = [part[0].shape[1] for part in right]

    def spec(rows):
        return pl.BlockSpec((1, rows, C), lambda g, _: (g, 0, 0))

    def both(groups):
        operands, specs = [], []
        for arrays in groups:
            for array in arrays:
                rows = array.shape[1]
                operands.append(array.reshape(2, 4, rows, C))
                specs.append(pl.BlockSpec((2, 1, rows, C), lambda g, _: (0, g, 0, 0)))
        return operands, specs

    left, left_specs = both(left)
    right, right_specs = both(right)
    out_spec = pl.BlockSpec((2, 1, 256, C), lambda g, _: (0, g, 0, 0))
    total, kept = call(
        functools.partial(near_kernel, left_rows, right_rows),
        index,
        left + right,
        (4,),
        left_specs + right_specs,
        [out_spec, out_spec],
        [f32(2, 4, 256, C)] * 2,
        11,
        [pltpu.VMEM((4, 3, 256, 768), jnp.bfloat16), pltpu.VMEM((3, 3, 768, C), jnp.bfloat16)],
    )
    return call(
        functools.partial(far_kernel, right_rows),
        index,
        [total, kept] + [array for pair in across for array in pair],
        (4,),
        [out_spec, out_spec] + [spec(rows) for rows in sizes for _ in range(2)],
        out_spec,
        f32(2, 4, 256, C),
        4,
        [pltpu.VMEM((1, 3, 256, 768), jnp.bfloat16), pltpu.VMEM((1, 3, 768, C), jnp.bfloat16)],
    )


def local(x):
    f = lax.axis_index("freq")
    y, x_lo = f // 2, f % 2
    z = lax.axis_index("row")
    col = lax.axis_index("col")
    one, two, three = tables()
    blocks = x.reshape(16, 4, 256, C)
    place = jnp.stack([f, y, x_lo, jnp.int32(R3 + R2)])

    def for_partner(index, x_ref, out_ref):
        rows = rows_at(HALF * (1 - index[2]), HALF)
        return [(x_ref.at[:, g, rows, :], out_ref.at[g]) for g in range(4)]

    def for_self(index, x_ref, out_ref):
        rows = rows_at(HALF * index[2], HALF)
        return [(x_ref.at[:, g, rows, :], out_ref.at[g, 0]) for g in range(4)]

    def for_z(index, x_ref, out_ref):
        return [(x_ref.at[:, g, rows_at(index[3], R1), :], out_ref.at[g]) for g in range(4)]

    def for_y(r):
        def views(index, x_ref, out_ref):
            rows = rows_at(R3 + QUARTER * ((index[1] + r) % 4), QUARTER)
            return [(x_ref.at[:, :, rows, :], out_ref)]

        return pack(place, blocks, views, 1, (16, 4, QUARTER, C), (16, 4, QUARTER, C), 2)

    third_far = shift(pack(place, blocks, for_partner, 4, (16, HALF, C), (4, 16, HALF, C), 3), "x_lo")
    first = exchange(pack(place, blocks, for_z, 4, (16, R1, C), (4, 16, R1, C), 5), "z")
    second = [shift(for_y(r), "y", r) for r in (1, 2, 3)]
    third = pack(place, blocks, for_self, 4, (16, HALF, C), (4, 2, 16, HALF, C), 3)
    second = dft_by_row(jnp.stack([4 * f + z, y]), two, blocks, second)
    first, second, third, third_far = together(first, second, third, third_far)

    third = exchange(join(third, third_far), "z")
    own2 = second[0] + shift(second[1], "x_lo")
    mine1, other1 = reduce_ring(dft_by_owner(place, one, first, 9), "y")
    mine1, other1, own2, third = together(mine1, other1, own2, third)

    own2 = jnp.sum(exchange(own2, "z"), axis=0)
    own1 = mine1 + shift(other1, "x_lo")
    below1, above1 = near_z(own1)
    far1 = shift(own1, "x_hi")
    mine3, other3 = reduce_ring(dft_by_owner(place, three, third.reshape(8, 16, HALF, C), 7), "y")
    own2 = exchange(own2.reshape(4, 8, QUARTER, C), "y")
    own2 = jnp.transpose(own2, (1, 0, 2, 3)).reshape(8, R2, C)
    across1 = across_z(below1, above1)
    below2, above2 = near_z(own2)
    mine3, other3, far1 = together(mine3, other3, far1)

    other3 = shift(other3, "x_lo")
    own3 = jnp.where(x_lo == 0, jnp.concatenate([mine3, other3], axis=1), jnp.concatenate([other3, mine3], axis=1))
    far2 = shift(own2, "x_hi")
    own3, below2, above2, across1 = together(own3, below2, above2, across1)

    below3, above3 = near_z(own3)
    across2 = across_z(below2, above2)
    far3 = shift(own3, "x_hi")
    below3, above3, far2, far3, across2 = together(below3, above3, far2, far3, across2)
    across3 = across_z(below3, above3)

    left = [[own, shift(own, "core"), far, shift(far, "core")] for own, far in ((own3, far3), (own2, far2), (own1, far1))]
    right = [(own3, above3, below3), (own2, above2, below2), (own1, above1, below1)]
    starts = (0, R3, R3 + R2)
    return product(jnp.stack([col, z]), left, right, [across3, across2, across1], starts, starts)


def solution(mesh):
    in_specs = (P(("freq", "row"), None, "col"),)
    out_specs = P(None, "freq", "row", "col")
    return jax.shard_map(local, mesh=mesh, in_specs=in_specs, out_specs=out_specs, check_vma=False)
```
